256 devices in a mesh: island: 16 (over y_hi, x, core), fsdp: 16 (over y_lo, z).
Axes of the slice: x: 4, y: 4 (y_hi: 2, y_lo: 2; y = y_hi * 2 + y_lo), z: 8, core: 2. Of those that a mesh axis runs over, the one named last changes fastest.
Arguments:
- normed: bfloat16 [2, 49152, 8192], P(None, ('island', 'fsdp')), may hold values from -6 to 6
- value_weight: bfloat16 [16, 8192, 512], P('island', 'fsdp'), may hold values from -0.0625 to 0.0625
- value_cotangent: bfloat16 [2, 49152, 512], P(None, ('island', 'fsdp')), may hold values from -0.079589844 to 0.079589844
- local_fragment: bfloat16 [16, 8192, 512], P('island', 'fsdp'), may hold values from -6 to 6
- global_fragment: float32 [8192, 512], P('fsdp'), may hold values from -6 to 6
- outer_momentum: float32 [8192, 512], P('fsdp', 'island'), may hold values from -3 to 3
Outputs:
- projected: bfloat16 [2, 49152, 512], P(None, ('island', 'fsdp'))
- value_grad: float32 [16, 8192, 512], P('island', 'fsdp')
- new_global: float32 [8192, 512], P('fsdp')
- new_momentum: float32 [8192, 512], P('fsdp', 'island')
The draws below stay inside these ranges and needn't reach their ends.
All inputs are finite; a program needn't handle non-finite values.
Results may differ from the reference program's by a relative error of at most 0.001.
Values may be sent and summed in bfloat16 or wider, within the bound.
No kernel may reach another device: no remote copies, remote signals or barrier semaphores. Data moves between devices by JAX's collectives and lax.ppermute only.
A program may use at most 128 MiB of HBM per device.

```python
import jax
import jax.numpy as jnp
from jax import lax

D = 8192
MICRO = 2
KV = 512
ISLANDS = 16
TOKENS = 49152


def steps_of(rng, extent, split, least, high):
    level, own = 1.0, jax.random.fold_in(rng, 6)
    for dim, parts in split:
        draws = jnp.exp(jax.random.uniform(jax.random.fold_in(own, dim), (parts,), jnp.float32, least / len(split), high / len(split)))
        level = level * jnp.repeat(draws, extent[dim] // parts).reshape([-1 if axis == dim else 1 for axis in range(len(extent))])
    return level


def normal_values(rng, shape, deviation, limit, cuts=(), kind=jnp.bfloat16):
    values = jax.random.normal(rng, shape, jnp.float32) * deviation
    if len(cuts) > 0:
        values = steps_of(rng, shape, cuts, -0.22, 0.18) * values
    return jnp.clip(values, min=-limit, max=limit).astype(kind)


def setup_inputs(seed: int = 0) -> dict:
    key_of = jax.random.split(jax.random.key(seed), 7)
    normed = normal_values(key_of[0], (MICRO, TOKENS, D), 1.0, 6.0, ((1, 256),))
    value_weight = normal_values(key_of[1], (ISLANDS, D, KV), D ** -0.5, 0.0625, ((0, 16), (1, 16)))
    value_cotangent = normal_values(key_of[2], (MICRO, TOKENS, KV), 0.0125, 0.079589844, ((1, 256),))
    local_fragment = normal_values(key_of[3], (ISLANDS, D, KV), 1.0, 6.0, ((0, 16), (1, 16)))
    global_fragment = normal_values(key_of[4], (D, KV), 1.0, 6.0, ((0, 16),), jnp.float32)
    outer_momentum = normal_values(key_of[5], (D, KV), 0.5, 3.0, ((0, 16), (1, 16)), jnp.float32)
    return dict(normed=normed, value_weight=value_weight, value_cotangent=value_cotangent, local_fragment=local_fragment, global_fragment=global_fragment, outer_momentum=outer_momentum)


outer_rate = 0.7
outer_mu = 0.9


def reference(normed, value_weight, value_cotangent, local_fragment, global_fragment, outer_momentum):
    island_rows = TOKENS // ISLANDS

    def per_island(island):
        offset = (island * island_rows).astype(jnp.int32)
        inputs = lax.dynamic_slice_in_dim(normed, offset, island_rows, 1).reshape(MICRO * island_rows, D)
        cotangents = lax.dynamic_slice_in_dim(value_cotangent, offset, island_rows, 1).reshape(MICRO * island_rows, KV)
        weights = lax.dynamic_index_in_dim(value_weight, island, 0, keepdims=False)
        outputs = jnp.dot(inputs, weights, preferred_element_type=jnp.float32).astype(jnp.bfloat16)
        gradient = lax.dot_general(inputs, cotangents, (((0,), (0,)), ((), ())), preferred_element_type=jnp.float32)
        return outputs.reshape(MICRO, island_rows, KV), gradient

    outputs, value_grad = lax.map(per_island, jnp.arange(ISLANDS, dtype=jnp.int32))
    projected = jnp.transpose(outputs, (1, 0, 2, 3)).reshape(MICRO, TOKENS, KV)
    pseudo = jnp.sum(global_fragment[None] - local_fragment.astype(jnp.float32), axis=0) / ISLANDS
    new_momentum = outer_mu * outer_momentum + pseudo
    new_global = global_fragment - outer_rate * (pseudo + outer_mu * new_momentum)
    return projected, value_grad, new_global, new_momentum
```

```python
import jax
import jax.numpy as jnp
from jax import lax
from jax.sharding import PartitionSpec as P

outer_rate = 0.7
outer_mu = 0.9

Z = 8
PAIR = [(i, (i + Z) % (2 * Z)) for i in range(2 * Z)]
UP = [(i, i // Z * Z + (i + 1) % Z) for i in range(2 * Z)]
DOWN = [(i, i // Z * Z + (i - 1) % Z) for i in range(2 * Z)]
ROWS = [list(range(Z)), list(range(Z, 2 * Z))]
ORDER = (4, -3, 3, -2, 2, -1, 1, 0)
f32 = jnp.float32


def xor(bit):
    return [(i, i ^ bit) for i in range(16)]


def after(x, *deps):
    return lax.optimization_barrier((x, *deps))[0]


def pick(a, i, axis):
    return lax.dynamic_index_in_dim(a, i, axis, keepdims=False)


def outer_step(local, global_fragment, outer_momentum):
    island = lax.axis_index("island").astype(jnp.uint32)
    bits = [(island >> b) & 1 for b in range(4)]
    cols = outer_momentum.shape[1]
    rows = local.shape[0]
    part = local.T.reshape(2, 2, 2, 2, cols, rows)
    for b in range(4):
        sent = pick(part, 1 - bits[b], 3 - b)
        part = pick(part, bits[b], 3 - b).astype(f32) + lax.ppermute(sent, "island", xor(1 << b)).astype(f32)
    mine = lax.dynamic_slice_in_dim(global_fragment, island * cols, cols, 1).T
    pseudo = mine - part / 16
    momentum = outer_mu * outer_momentum.T + pseudo
    full = mine - outer_rate * (pseudo + outer_mu * momentum)
    for b in (3, 2, 1, 0):
        got = lax.ppermute(full, "island", xor(1 << b))
        low = bits[b] == 0
        full = jnp.stack([jnp.where(low, full, got), jnp.where(low, got, full)], 3 - b)
    return full.reshape(-1, rows).T, momentum.T


def per_device(
    normed, value_weight, value_cotangent, local_fragment, global_fragment, outer_momentum
):
    micro_count, tok_rows, model_width = normed.shape
    kv = value_cotangent.shape[2]
    tokens = micro_count * tok_rows
    half = model_width // 2
    chunk = half // Z
    n = normed.reshape(tokens, model_width)
    c = value_cotangent.reshape(tokens, kv)
    fsdp = lax.axis_index("fsdp").astype(jnp.uint32)
    yl, z = fsdp >> 3, fsdp & 7
    spots = [((z + (o & 7)) & 7) * chunk for o in ORDER]

    w_half = lax.all_gather(value_weight[0], "fsdp", axis=0, tiled=True, axis_index_groups=ROWS)

    c_p = lax.ppermute(c, "fsdp", PAIR)
    got = []
    for s in range(Z):
        cut = lax.dynamic_slice_in_dim(n, (1 - yl) * half + spots[s], chunk, 1)
        if s >= 2:
            cut = after(cut, got[s - 2])
        elif s == 1:
            cut = after(cut, c_p)
        got.append(lax.ppermute(cut, "fsdp", PAIR))

    bound = jnp.max(jnp.abs(n)).astype(f32) * jnp.max(jnp.abs(c)).astype(f32)
    bound = jnp.full((8, 128), bound)
    for perm in (PAIR, xor(1), xor(2), xor(4)):
        bound = jnp.maximum(bound, lax.ppermute(bound, "fsdp", perm))
    bound = jnp.maximum(bound[0, 0] * (tokens * 2 * Z), 1e-33)
    scale, unscale = 32768.0 / bound, bound / 32768.0

    def tn(a, b):
        return lax.dot_general(a, b, (((0,), (0,)), ((), ())), preferred_element_type=f32)

    n_half = lax.dynamic_slice_in_dim(n, yl * half, half, 1)
    own = tn(n_half, c)
    up = down = None
    for s in range(Z):
        g = lax.dynamic_slice_in_dim(own, spots[s], chunk, 0) + tn(got[s], c_p)
        g = g * scale
        o = ORDER[s]
        if o > 0:
            if up is not None:
                g = g + up.astype(f32)
            up = lax.ppermute(g.astype(jnp.float16), "fsdp", UP)
        elif o < 0:
            if down is not None:
                g = g + down.astype(f32)
            down = lax.ppermute(g.astype(jnp.float16), "fsdp", DOWN)
        else:
            g = g + up.astype(f32) + down.astype(f32)
    value_grad = (g * unscale)[None]

    theirs = jnp.zeros((tokens, kv), f32)
    for s in range(Z):
        ws = lax.dynamic_slice_in_dim(w_half, spots[s], chunk, 0)
        theirs = theirs + jnp.dot(got[s], ws, preferred_element_type=f32)
    mine = jnp.dot(n_half, w_half, preferred_element_type=f32)
    projected = mine + lax.ppermute(theirs, "fsdp", PAIR)
    projected = projected.astype(jnp.bfloat16).reshape(micro_count, tok_rows, kv)

    new_global, new_momentum = outer_step(local_fragment[0], global_fragment, outer_momentum)
    return (projected, value_grad, new_global, new_momentum)


def solution(mesh):
    placed = (
        P(None, ("island", "fsdp"), None),
        P("island", "fsdp", None),
        P(None, ("island", "fsdp"), None),
        P("island", "fsdp", None),
        P("fsdp", None),
        P("fsdp", "island"),
    )
    return jax.shard_map(
        per_device,
        mesh=mesh,
        in_specs=placed,
        out_specs=(
            P(None, ("island", "fsdp"), None),
            P("island", "fsdp", None),
            P("fsdp", None),
            P("fsdp", "island"),
        ),
        check_vma=False,
    )
```

```python
import jax
import jax.numpy as jnp
from jax import lax
from jax.sharding import PartitionSpec as P

outer_rate = 0.7
outer_mu = 0.9

Z = 8
PAIR = [(i, (i + Z) % (2 * Z)) for i in range(2 * Z)]
UP = [(i, i // Z * Z + (i + 1) % Z) for i in range(2 * Z)]
DOWN = [(i, i // Z * Z + (i - 1) % Z) for i in range(2 * Z)]
ORDER = (4, -3, 3, -2, 2, -1, 1, 0)
f32 = jnp.float32
LIMIT = 6144 * 6 * 0.0796
PACK = 65000.0**2 / LIMIT


def coded(x):
    root = jnp.sqrt(jnp.abs(x) * PACK)
    return jnp.where(x < 0, -root, root).astype(jnp.float16)


def decoded(x):
    x = x.astype(f32)
    return x * jnp.abs(x) * (1 / PACK)


def xor(bit):
    return [(i, i ^ bit) for i in range(16)]


def after(x, *deps):
    return lax.optimization_barrier((x, *deps))[0]


def pick(a, i, axis):
    return lax.dynamic_index_in_dim(a, i, axis, keepdims=False)


class Order:
    def __init__(self):
        self.last = ()

    def gate(self, *xs):
        if not self.last:
            return xs if len(xs) > 1 else xs[0]
        out = lax.optimization_barrier((*xs, *self.last))
        return out[: len(xs)] if len(xs) > 1 else out[0]

    def done(self, *xs):
        self.last = xs


def per_device(
    normed, value_weight, value_cotangent, local_fragment, global_fragment, outer_momentum
):
    micro_count, tok_rows, model_width = normed.shape
    kv = value_cotangent.shape[2]
    tokens = micro_count * tok_rows
    half = model_width // 2
    chunk = half // Z
    n = normed.reshape(tokens, model_width)
    c = value_cotangent.reshape(tokens, kv)
    fsdp = lax.axis_index("fsdp").astype(jnp.uint32)
    yl, z = fsdp >> 3, fsdp & 7
    spots = [((z + (o & 7)) & 7) * chunk for o in ORDER]
    order = Order()

    def cut(s, side):
        return lax.dynamic_slice_in_dim(n, side * half + spots[s], chunk, 1)

    def tn(a, b):
        return lax.dot_general(a, b, (((0,), (0,)), ((), ())), preferred_element_type=f32)

    def over_y(x):
        return lax.ppermute(x, "fsdp", PAIR)

    island = lax.axis_index("island").astype(jnp.uint32)
    bits = [(island >> b) & 1 for b in range(4)]
    cols = outer_momentum.shape[1]
    rows = global_fragment.shape[0]

    def fold_send(part, b):
        return lax.ppermute(pick(part, 1 - bits[b], 3 - b), "island", xor(1 << b))

    def fold(part, got, b):
        return pick(part, bits[b], 3 - b).astype(f32) + got.astype(f32)

    def spread_send(full, b):
        return lax.ppermute(full, "island", xor(1 << b))

    def spread(full, got, b):
        low = bits[b] == 0
        return jnp.stack([jnp.where(low, full, got), jnp.where(low, got, full)], 3 - b)

    c_p = over_y(c)
    w = {0: value_weight[0]}

    def w_hop(way, h):
        w[-way * h] = lax.ppermute(w[-way * (h - 1)], "fsdp", UP if way > 0 else DOWN)

    def next_w(way, h):
        w[-way * h] = order.gate(w[-way * h])
        w_hop(way, h + 1)
        order.done(w[-way * h])

    send = [cut(s, 1 - yl) for s in range(Z)]
    order.done(*send)
    k = [None] * Z
    k[0] = over_y(send[0])
    w[0] = order.gate(w[0])
    w_hop(1, 1)
    w_hop(-1, 1)
    own = [None] * Z

    def own_dots(*steps):
        cc = order.gate(c)
        for s in steps:
            own[s] = tn(ours[s], cc)
        order.done(*[own[s] for s in steps])

    full = None

    def fold_step(b):
        nonlocal part, sent
        sent, part = order.gate(sent, part)
        part = fold(part, sent, b)
        if b < 3:
            sent = fold_send(part, b + 1)
        order.done(part)

    def spread_step(b):
        nonlocal full, sent
        sent, full = order.gate(sent, full)
        full = spread(full, sent, b)
        if b > 0:
            sent = spread_send(full, b - 1)
        order.done(full)

    carry = {1: None, -1: None}

    def ring(s):
        got, mine, cc = order.gate(k[s], own[s], c_p)
        g = mine + tn(got, cc)
        o = ORDER[s]
        if o == 0:
            g = g + decoded(carry[1]) + decoded(carry[-1])
            order.done(g)
            return g
        way = 1 if o > 0 else -1
        if carry[way] is not None:
            g = g + decoded(carry[way])
        g = coded(g)
        order.done(g)
        carry[way] = lax.ppermute(g, "fsdp", UP if way > 0 else DOWN)

    def next_chunk(s):
        if s + 3 < Z:
            k[s], send[s + 3] = order.gate(k[s], send[s + 3])
            k[s + 3] = over_y(send[s + 3])
            order.done(k[s], send[s + 3])

    def start_chunk(s, *deps):
        out = order.gate(send[s], *deps)
        send[s] = out[0] if deps else out
        k[s] = over_y(send[s])
        order.done(send[s], *out[1:] if deps else ())

    def theirs(steps, so_far):
        return products(k, steps, so_far)

    def products(blocks, steps, so_far):
        gated = order.gate(*[blocks[s] for s in steps], *[w[ORDER[s]] for s in steps])
        for got, rows_w in zip(gated[: len(steps)], gated[len(steps) :]):
            d = jnp.dot(got, rows_w, preferred_element_type=f32)
            so_far = d if so_far is None else so_far + d
        order.done(so_far)
        return so_far

    local = order.gate(local_fragment[0])
    part = local.T.reshape(2, 2, 2, 2, cols, rows)
    sent = fold_send(part, 0)
    order.done(part)
    n, c_p = order.gate(n, c_p)
    ours = [cut(s, yl) for s in range(Z)]
    order.done(*ours)
    start_chunk(1)
    next_w(1, 1)
    next_w(-1, 1)
    own_dots(0)
    start_chunk(2)
    ring(0)
    fold_step(0)
    own_dots(1, 2)
    next_chunk(0)
    next_chunk(1)
    ring(1)
    next_w(1, 2)
    next_w(-1, 2)
    fold_step(1)
    next_chunk(2)
    ring(2)
    own_dots(3)
    next_chunk(3)
    ring(3)
    fold_step(2)
    next_w(-1, 3)
    next_chunk(4)
    partner = theirs((2, 3, 4), None)
    own_dots(4)
    ring(4)
    own_dots(5)
    ring(5)
    fold_step(3)
    mine = lax.dynamic_slice_in_dim(global_fragment.T, island * cols, cols, 0)
    pseudo = mine - part / 16
    momentum = outer_mu * outer_momentum.T + pseudo
    full = mine - outer_rate * (pseudo + outer_mu * momentum)
    sent = spread_send(full, 3)
    order.done(full)
    own_dots(6)
    partner = theirs((1, 5), partner)
    ring(6)
    partner = theirs((0, 6), partner)
    partner = theirs((7,), partner)
    back = over_y(partner)
    spread_step(3)
    forward = products(ours, range(Z), None)
    spread_step(2)
    own_dots(7)
    spread_step(1)
    value_grad = ring(7)[None]
    spread_step(0)
    new_global = full.reshape(-1, rows).T
    order.done(new_global)
    back, forward = order.gate(back, forward)
    projected = (forward + back).astype(jnp.bfloat16).reshape(micro_count, tok_rows, kv)
    return (projected, value_grad, new_global, momentum.T)


def solution(mesh):
    placed = (
        P(None, ("island", "fsdp"), None),
        P("island", "fsdp", None),
        P(None, ("island", "fsdp"), None),
        P("island", "fsdp", None),
        P("fsdp", None),
        P("fsdp", "island"),
    )
    return jax.shard_map(
        per_device,
        mesh=mesh,
        in_specs=placed,
        out_specs=(
            P(None, ("island", "fsdp"), None),
            P("island", "fsdp", None),
            P("fsdp", None),
            P("fsdp", "island"),
        ),
        check_vma=False,
    )
```

```python
import jax
import jax.numpy as jnp
from jax import lax
from jax.sharding import PartitionSpec as P

outer_rate = 0.7
outer_mu = 0.9

Z = 8
PAIR = [(i, (i + Z) % (2 * Z)) for i in range(2 * Z)]
UP = [(i, i // Z * Z + (i + 1) % Z) for i in range(2 * Z)]
DOWN = [(i, i // Z * Z + (i - 1) % Z) for i in range(2 * Z)]
ORDER = (4, -3, 3, -2, 2, -1, 1, 0)
f32 = jnp.float32
LIMIT = 6144 * 6 * 0.0796
PACK = 65000.0**2 / LIMIT


def coded(x):
    root = jnp.sqrt(jnp.abs(x) * PACK)
    return jnp.where(x < 0, -root, root).astype(jnp.float16)


def decoded(x):
    x = x.astype(f32)
    return x * jnp.abs(x) * (1 / PACK)


def xor(bit):
    return [(i, i ^ bit) for i in range(16)]


def after(x, *deps):
    return lax.optimization_barrier((x, *deps))[0]


def pick(a, i, axis):
    return lax.dynamic_index_in_dim(a, i, axis, keepdims=False)


class Order:
    def __init__(self):
        self.last = ()

    def gate(self, *xs):
        if not self.last:
            return xs if len(xs) > 1 else xs[0]
        out = lax.optimization_barrier((*xs, *self.last))
        return out[: len(xs)] if len(xs) > 1 else out[0]

    def done(self, *xs):
        self.last = xs


def per_device(
    normed, value_weight, value_cotangent, local_fragment, global_fragment, outer_momentum
):
    micro_count, tok_rows, model_width = normed.shape
    kv = value_cotangent.shape[2]
    tokens = micro_count * tok_rows
    half = model_width // 2
    chunk = half // Z
    n = normed.reshape(tokens, model_width)
    c = value_cotangent.reshape(tokens, kv)
    fsdp = lax.axis_index("fsdp").astype(jnp.uint32)
    yl, z = fsdp >> 3, fsdp & 7
    spots = [((z + (o & 7)) & 7) * chunk for o in ORDER]
    order = Order()

    def cut(s, side):
        return lax.dynamic_slice_in_dim(n, side * half + spots[s], chunk, 1)

    def tn(a, b):
        return lax.dot_general(a, b, (((0,), (0,)), ((), ())), preferred_element_type=f32)

    def over_y(x):
        return lax.ppermute(x, "fsdp", PAIR)

    island = lax.axis_index("island").astype(jnp.uint32)
    bits = [(island >> b) & 1 for b in range(4)]
    cols = outer_momentum.shape[1]
    rows = global_fragment.shape[0]

    def fold_send(part, b):
        return lax.ppermute(pick(part, 1 - bits[b], 3 - b), "island", xor(1 << b))

    def fold(part, got, b):
        return pick(part, bits[b], 3 - b).astype(f32) + got.astype(f32)

    def spread_send(full, b):
        return lax.ppermute(full, "island", xor(1 << b))

    def spread(full, got, b):
        low = bits[b] == 0
        return jnp.stack([jnp.where(low, full, got), jnp.where(low, got, full)], 3 - b)

    c_p = over_y(c)
    w = {0: value_weight[0]}

    def w_hop(way, h):
        w[-way * h] = lax.ppermute(w[-way * (h - 1)], "fsdp", UP if way > 0 else DOWN)

    def next_w(way, h):
        w[-way * h] = order.gate(w[-way * h])
        w_hop(way, h + 1)
        order.done(w[-way * h])

    send = [cut(s, 1 - yl) for s in range(Z)]
    order.done(*send)
    k = [None] * Z
    k[0] = over_y(send[0])
    w[0] = order.gate(w[0])
    w_hop(1, 1)
    w_hop(-1, 1)
    own = [None] * Z

    def own_dots(*steps):
        cc = order.gate(c)
        for s in steps:
            own[s] = tn(ours[s], cc)
        order.done(*[own[s] for s in steps])

    full = None

    def fold_step(b):
        nonlocal part, sent
        sent, part = order.gate(sent, part)
        part = fold(part, sent, b)
        if b < 2:
            sent = fold_send(part, b + 1)
        else:
            part = jnp.concatenate([part.reshape(2 * cols, rows), outer_momentum.T], 0)
            sent = spread_send(part, 3)
        order.done(part)

    def outer_step():
        nonlocal part, sent
        sent, part = order.gate(sent, part)
        total = part[: 2 * cols] + sent[: 2 * cols]
        low = bits[3] == 0
        momentum = jnp.concatenate(
            [jnp.where(low, part[2 * cols :], sent[2 * cols :]), jnp.where(low, sent[2 * cols :], part[2 * cols :])], 0
        )
        both = global_fragment.T.reshape(2, 8, cols, rows)
        mine = pick(both, island & 7, 1).reshape(2 * cols, rows)
        pseudo = mine - total / 16
        momentum = outer_mu * momentum + pseudo
        new = mine - outer_rate * (pseudo + outer_mu * momentum)
        order.done(new)
        return new.reshape(2, cols, rows), pick(momentum.reshape(2, cols, rows), bits[3], 0)

    def spread_step(b):
        nonlocal full, sent
        sent, full = order.gate(sent, full)
        full = spread(full, sent, b)
        if b > 0:
            sent = spread_send(full, b - 1)
        order.done(full)

    carry = {1: None, -1: None}

    def ring(s):
        got, mine, cc = order.gate(k[s], own[s], c_p)
        g = mine + tn(got, cc)
        o = ORDER[s]
        if o == 0:
            g = g + decoded(carry[1]) + decoded(carry[-1])
            order.done(g)
            return g
        way = 1 if o > 0 else -1
        if carry[way] is not None:
            g = g + decoded(carry[way])
        g = coded(g)
        order.done(g)
        carry[way] = lax.ppermute(g, "fsdp", UP if way > 0 else DOWN)

    def next_chunk(s):
        if s + 3 < Z:
            k[s], send[s + 3] = order.gate(k[s], send[s + 3])
            k[s + 3] = over_y(send[s + 3])
            order.done(k[s], send[s + 3])

    def start_chunk(s, *deps):
        out = order.gate(send[s], *deps)
        send[s] = out[0] if deps else out
        k[s] = over_y(send[s])
        order.done(send[s], *out[1:] if deps else ())

    def theirs(steps, so_far):
        return products(k, steps, so_far)

    def products(blocks, steps, so_far):
        gated = order.gate(*[blocks[s] for s in steps], *[w[ORDER[s]] for s in steps])
        for got, rows_w in zip(gated[: len(steps)], gated[len(steps) :]):
            d = jnp.dot(got, rows_w, preferred_element_type=f32)
            so_far = d if so_far is None else so_far + d
        order.done(so_far)
        return so_far

    local = order.gate(local_fragment[0])
    part = local.T.reshape(2, 2, 2, 2, cols, rows)
    sent = fold_send(part, 0)
    order.done(part)
    n, c_p = order.gate(n, c_p)
    ours = [cut(s, yl) for s in range(Z)]
    order.done(*ours)
    start_chunk(1)
    next_w(1, 1)
    next_w(-1, 1)
    own_dots(0)
    start_chunk(2)
    ring(0)
    fold_step(0)
    own_dots(1, 2)
    next_chunk(0)
    next_chunk(1)
    ring(1)
    next_w(1, 2)
    next_w(-1, 2)
    fold_step(1)
    next_chunk(2)
    ring(2)
    own_dots(3)
    next_chunk(3)
    ring(3)
    fold_step(2)
    next_w(-1, 3)
    next_chunk(4)
    partner = theirs((2, 3, 4), None)
    own_dots(4)
    ring(4)
    own_dots(5)
    ring(5)
    own_dots(6)
    partner = theirs((1, 5), partner)
    ring(6)
    partner = theirs((0, 6), partner)
    partner = theirs((7,), partner)
    back = over_y(partner)
    full, momentum = outer_step()
    sent = spread_send(full, 2)
    forward = products(ours, range(Z), None)
    spread_step(2)
    own_dots(7)
    spread_step(1)
    value_grad = ring(7)[None]
    spread_step(0)
    new_global = full.reshape(-1, rows).T
    order.done(new_global)
    back, forward = order.gate(back, forward)
    projected = (forward + back).astype(jnp.bfloat16).reshape(micro_count, tok_rows, kv)
    return (projected, value_grad, new_global, momentum.T)


def solution(mesh):
    placed = (
        P(None, ("island", "fsdp"), None),
        P("island", "fsdp", None),
        P(None, ("island", "fsdp"), None),
        P("island", "fsdp", None),
        P("fsdp", None),
        P("fsdp", "island"),
    )
    return jax.shard_map(
        per_device,
        mesh=mesh,
        in_specs=placed,
        out_specs=(
            P(None, ("island", "fsdp"), None),
            P("island", "fsdp", None),
            P("fsdp", None),
            P("fsdp", "island"),
        ),
        check_vma=False,
    )
```

```python
import jax
import jax.numpy as jnp
from jax import lax
from jax.sharding import PartitionSpec as P

outer_rate = 0.7
outer_mu = 0.9

Z = 8
PAIR = [(i, (i + Z) % (2 * Z)) for i in range(2 * Z)]
UP = [(i, i // Z * Z + (i + 1) % Z) for i in range(2 * Z)]
DOWN = [(i, i // Z * Z + (i - 1) % Z) for i in range(2 * Z)]
ORDER = (4, -3, 3, -2, 2, -1, 1, 0)
f32 = jnp.float32
LIMIT = 6144 * 6 * 0.0796
PACK = 65000.0**2 / LIMIT


def coded(x):
    root = jnp.sqrt(jnp.abs(x) * PACK)
    return jnp.where(x < 0, -root, root).astype(jnp.float16)


def decoded(x):
    x = x.astype(f32)
    return x * jnp.abs(x) * (1 / PACK)


def xor(bit):
    return [(i, i ^ bit) for i in range(16)]


def after(x, *deps):
    return lax.optimization_barrier((x, *deps))[0]


def pick(a, i, axis):
    return lax.dynamic_index_in_dim(a, i, axis, keepdims=False)


class Order:
    def __init__(self):
        self.last = ()

    def gate(self, *xs):
        if not self.last:
            return xs if len(xs) > 1 else xs[0]
        out = lax.optimization_barrier((*xs, *self.last))
        return out[: len(xs)] if len(xs) > 1 else out[0]

    def done(self, *xs):
        self.last = xs


def per_device(
    normed, value_weight, value_cotangent, local_fragment, global_fragment, outer_momentum
):
    micro_count, tok_rows, model_width = normed.shape
    kv = value_cotangent.shape[2]
    tokens = micro_count * tok_rows
    half = model_width // 2
    chunk = half // Z
    n = normed.reshape(tokens, model_width)
    c = value_cotangent.reshape(tokens, kv)
    fsdp = lax.axis_index("fsdp").astype(jnp.uint32)
    yl, z = fsdp >> 3, fsdp & 7
    spots = [((z + (o & 7)) & 7) * chunk for o in ORDER]
    order = Order()

    def cut(s, side):
        return lax.dynamic_slice_in_dim(n, side * half + spots[s], chunk, 1)

    def tn(a, b):
        return lax.dot_general(a, b, (((0,), (0,)), ((), ())), preferred_element_type=f32)

    def over_y(x):
        return lax.ppermute(x, "fsdp", PAIR)

    island = lax.axis_index("island").astype(jnp.uint32)
    bits = [(island >> b) & 1 for b in range(4)]
    cols = outer_momentum.shape[1]
    rows = global_fragment.shape[0]

    def fold_send(part, b):
        return lax.ppermute(pick(part, 1 - bits[b], 3 - b), "island", xor(1 << b))

    def fold(part, got, b):
        return pick(part, bits[b], 3 - b).astype(f32) + got.astype(f32)

    def spread_send(full, b):
        return lax.ppermute(full, "island", xor(1 << b))

    def spread(full, got, b):
        low = bits[b] == 0
        return jnp.stack([jnp.where(low, full, got), jnp.where(low, got, full)], 3 - b)

    c_p = over_y(c)
    w = {0: value_weight[0]}

    def w_hop(way, h):
        w[-way * h] = lax.ppermute(w[-way * (h - 1)], "fsdp", UP if way > 0 else DOWN)

    def next_w(way, h):
        w[-way * h] = order.gate(w[-way * h])
        w_hop(way, h + 1)
        order.done(w[-way * h])

    send = [cut(s, 1 - yl) for s in range(Z)]
    order.done(*send)
    k = [None] * Z
    k[0] = over_y(send[0])
    w[0] = order.gate(w[0])
    w_hop(1, 1)
    w_hop(-1, 1)
    own = [None] * Z

    def own_dots(*steps):
        cc = order.gate(c)
        for s in steps:
            own[s] = tn(ours[s], cc)
        order.done(*[own[s] for s in steps])

    full = None

    def fold_step(b):
        nonlocal part, sent
        sent, part = order.gate(sent, part)
        part = fold(part, sent, b)
        if b < 2:
            sent = fold_send(part, b + 1)
        else:
            part = jnp.concatenate([part.reshape(2 * cols, rows), outer_momentum.T], 0)
            sent = spread_send(part, 3)
        order.done(part)

    def outer_step():
        nonlocal part, sent
        sent, part = order.gate(sent, part)
        total = part[: 2 * cols] + sent[: 2 * cols]
        low = bits[3] == 0
        momentum = jnp.concatenate(
            [jnp.where(low, part[2 * cols :], sent[2 * cols :]), jnp.where(low, sent[2 * cols :], part[2 * cols :])], 0
        )
        both = global_fragment.T.reshape(2, 8, cols, rows)
        mine = pick(both, island & 7, 1).reshape(2 * cols, rows)
        pseudo = mine - total / 16
        momentum = outer_mu * momentum + pseudo
        new = mine - outer_rate * (pseudo + outer_mu * momentum)
        order.done(new)
        return new.reshape(2, cols, rows), pick(momentum.reshape(2, cols, rows), bits[3], 0)

    def spread_step(b):
        nonlocal full, sent
        sent, full = order.gate(sent, full)
        full = spread(full, sent, b)
        if b > 0:
            sent = spread_send(full, b - 1)
        order.done(full)

    carry = {1: None, -1: None}

    def ring(s):
        got, mine, cc = order.gate(k[s], own[s], c_p)
        g = mine + tn(got, cc)
        o = ORDER[s]
        if o == 0:
            g = g + decoded(carry[1]) + decoded(carry[-1])
            order.done(g)
            return g
        way = 1 if o > 0 else -1
        if carry[way] is not None:
            g = g + decoded(carry[way])
        g = coded(g)
        order.done(g)
        carry[way] = lax.ppermute(g, "fsdp", UP if way > 0 else DOWN)

    def next_chunk(s):
        if s + 3 < Z:
            k[s], send[s + 3] = order.gate(k[s], send[s + 3])
            k[s + 3] = over_y(send[s + 3])
            order.done(k[s], send[s + 3])

    def start_chunk(s, *deps):
        out = order.gate(send[s], *deps)
        send[s] = out[0] if deps else out
        k[s] = over_y(send[s])
        order.done(send[s], *out[1:] if deps else ())

    def theirs(steps, so_far):
        return products(k, steps, so_far)

    def products(blocks, steps, so_far):
        gated = order.gate(*[blocks[s] for s in steps], *[w[ORDER[s]] for s in steps])
        for got, rows_w in zip(gated[: len(steps)], gated[len(steps) :]):
            d = jnp.dot(got, rows_w, preferred_element_type=f32)
            so_far = d if so_far is None else so_far + d
        order.done(so_far)
        return so_far

    local = order.gate(local_fragment[0])
    part = local.T.reshape(2, 2, 2, 2, cols, rows)
    sent = fold_send(part, 0)
    order.done(part)
    n, c_p = order.gate(n, c_p)
    ours = [cut(s, yl) for s in range(Z)]
    order.done(*ours)
    start_chunk(1)
    next_w(1, 1)
    next_w(-1, 1)
    own_dots(0)
    start_chunk(2)
    ring(0)
    fold_step(0)
    own_dots(1, 2)
    next_chunk(0)
    next_chunk(1)
    ring(1)
    next_w(1, 2)
    next_w(-1, 2)
    fold_step(1)
    next_chunk(2)
    ring(2)
    own_dots(3)
    next_chunk(3)
    ring(3)
    fold_step(2)
    next_w(-1, 3)
    next_chunk(4)
    partner = theirs((2, 3, 4), None)
    own_dots(4)
    ring(4)
    w[-3] = order.gate(w[-3])
    order.done(w[-3])
    own_dots(5)
    ring(5)
    own_dots(6)
    partner = theirs((1, 5), partner)
    ring(6)
    partner = theirs((0, 6), partner)
    partner = theirs((7,), partner)
    back = over_y(partner)
    full, momentum = outer_step()
    sent = spread_send(full, 2)
    forward = products(ours, range(Z), None)
    spread_step(2)
    own_dots(7)
    spread_step(1)
    value_grad = ring(7)[None]
    spread_step(0)
    new_global = full.reshape(-1, rows).T
    order.done(new_global)
    back, forward = order.gate(back, forward)
    projected = (forward + back).astype(jnp.bfloat16).reshape(micro_count, tok_rows, kv)
    return (projected, value_grad, new_global, momentum.T)


def solution(mesh):
    placed = (
        P(None, ("island", "fsdp"), None),
        P("island", "fsdp", None),
        P(None, ("island", "fsdp"), None),
        P("island", "fsdp", None),
        P("fsdp", None),
        P("fsdp", "island"),
    )
    return jax.shard_map(
        per_device,
        mesh=mesh,
        in_specs=placed,
        out_specs=(
            P(None, ("island", "fsdp"), None),
            P("island", "fsdp", None),
            P("fsdp", None),
            P("fsdp", "island"),
        ),
        check_vma=False,
    )
```
